512 devices in a mesh: dp: 64 (over z_hi, x, y), tensor: 8 (over z_lo, core).
Axes of the slice: x: 4, y: 8, z: 8 (z_hi: 2, z_lo: 4; z = z_hi * 4 + z_lo), core: 2. Of those that a mesh axis runs over, the one named last changes fastest.
Arguments:
- hidden_act: bfloat16 [24576, 36864], P('dp', 'tensor'), may hold values from -64 to 64
- out_grad: bfloat16 [24576, 4608], P('dp', 'tensor'), may hold values from -0.00012529303 to 0.00012529303
- privacy_noise: float32 [4608, 1024], P('dp', 'tensor'), may hold values from -4 to 4
Outputs:
- update: float32 [4608, 1024], P('dp', 'tensor')
- mean_sq_norm: float32 [], replicated
The draws below stay inside these ranges and needn't reach their ends.
All inputs are finite; a program needn't handle non-finite values.
Results may differ from the reference program's by a relative error of at most 0.0003.
Values may be sent and summed in bfloat16 or wider, within the bound.
A program may use at most 64 MiB of HBM per device.

```python
import math
import jax
import jax.numpy as jnp
from jax import lax

D = 4608
FF = 36864
SEQ = 384
BLOCK = 128
BATCH = 64
TOKENS = 24576
N_TENSOR = 8


def draw_hidden_act(key, part):
    key = jax.random.fold_in(key, 7)
    keys = jax.random.split(key, 5)
    rough = jax.random.normal(keys[0], (BATCH, SEQ, FF), jnp.float32)
    share = 0.1
    tilt = 0.55
    common = jax.random.normal(keys[1], (BATCH, 1, FF), jnp.float32)
    base = jnp.clip(math.sqrt(1.0 - share) * rough + math.sqrt(share) * common, -4.0, 4.0)
    place = jnp.arange(FF, dtype=jnp.float32) / max(FF - 1, 1)
    column = jnp.exp(jax.random.uniform(keys[2], (FF,), jnp.float32, 0.0, math.log(10.0))) / 4.64
    column = column * jnp.exp(tilt * place)
    token = jnp.exp(jax.random.uniform(keys[3], (BATCH, SEQ, 1), jnp.float32, 0.0, math.log(10.0))) / 4.64
    order = jnp.arange(BATCH, dtype=jnp.float32) / max(BATCH - 1, 1)
    example = jnp.exp(jax.random.uniform(keys[4], (BATCH, 1, 1), jnp.float32, math.log(0.2), math.log(5.0)))
    example = example * jnp.exp(0.55 * order)[:, None, None]
    values = base * column * token * example
    return jnp.clip(values, -64.0, 64.0).reshape(TOKENS, FF).astype(jnp.bfloat16)


def draw_out_grad(key, part):
    key = jax.random.fold_in(key, 13)
    keys = jax.random.split(key, 4)
    rough = jax.random.normal(keys[0], (BATCH, SEQ, D), jnp.float32)
    share = 0.1
    tilt = 0.55
    common = jax.random.normal(keys[1], (BATCH, 1, D), jnp.float32)
    base = jnp.clip(math.sqrt(1.0 - share) * rough + math.sqrt(share) * common, -4.0, 4.0)
    place = jnp.arange(D, dtype=jnp.float32) / max(D - 1, 1)
    column = jnp.exp(jax.random.uniform(keys[2], (D,), jnp.float32, 0.0, math.log(10.0))) / 4.64
    column = column * jnp.exp(tilt * place)
    token = jnp.exp(jax.random.uniform(keys[3], (BATCH, SEQ, 1), jnp.float32, 0.0, math.log(10.0))) / 4.64
    unit = (SEQ * FF * D) ** (-0.5)
    values = base * column * token * (0.5 * unit)
    return jnp.clip(values, -32.0 * unit, 32.0 * unit).reshape(TOKENS, D).astype(jnp.bfloat16)


def block_scale(key, extent, pieces, least, top_value):
    factor_of, own = 1.0, jax.random.fold_in(key, 6)
    for position, parts in pieces:
        steps = jnp.exp(jax.random.uniform(jax.random.fold_in(own, position), (parts,), jnp.float32, least / len(pieces), top_value / len(pieces)))
        factor_of = factor_of * jnp.repeat(steps, extent[position] // parts).reshape([-1 if axis == position else 1 for axis in range(len(extent))])
    return factor_of


def centred(stream_key, shape, scale, most, shards=(), kind=jnp.bfloat16):
    result = scale * jax.random.normal(stream_key, shape, jnp.float32)
    if shards:
        result = result * block_scale(stream_key, shape, shards, -0.22, 0.18)
    return jnp.clip(result, -most, most).astype(kind)


def setup_inputs(seed: int = 0) -> dict:
    arg_keys = jax.random.split(jax.random.key(seed), 4)
    return {
        "hidden_act": draw_hidden_act(jax.random.fold_in(arg_keys[3], 71), 0),
        "out_grad": draw_out_grad(jax.random.fold_in(arg_keys[3], 71), 0),
        "privacy_noise": centred(arg_keys[2], (D, N_TENSOR * BLOCK), 0.3, 4.0, ((0, 64), (1, 8)), jnp.float32),
    }


def reference(hidden_act, out_grad, privacy_noise):
    span = FF // N_TENSOR
    window = hidden_act.reshape(TOKENS, N_TENSOR, span)[:, :, :BLOCK].reshape(TOKENS, N_TENSOR * BLOCK)
    acts = hidden_act.reshape(BATCH, SEQ, FF)
    grads = out_grad.reshape(BATCH, SEQ, D)
    windows = window.reshape(BATCH, SEQ, N_TENSOR * BLOCK)

    def norm_of(pair):
        act, grad = pair
        act_gram = jnp.dot(act, act.T, preferred_element_type=jnp.float32)
        grad_gram = jnp.dot(grad, grad.T, preferred_element_type=jnp.float32)
        return jnp.sum(act_gram * grad_gram)
    sq_norm = lax.map(norm_of, (acts, grads))
    factor = 1.0 / jnp.maximum(jnp.sqrt(sq_norm), 1.0)

    def add_example(total, item):
        grad, win, weight = item
        bucket = jnp.dot(grad.T, win, preferred_element_type=jnp.float32)
        return (total + weight * bucket, None)
    start = jnp.zeros((D, N_TENSOR * BLOCK), jnp.float32)
    summed, _ = lax.scan(add_example, start, (grads, windows, factor))
    update = math.sqrt(FF * D / BATCH) * summed + privacy_noise
    mean_sq_norm = jnp.sum(sq_norm) / BATCH
    return (update, mean_sq_norm)
```

```python
import math

import jax
import jax.numpy as jnp
from jax import lax
from jax.experimental import pallas as pl
from jax.experimental.pallas import tpu as pltpu
from jax.sharding import PartitionSpec as P

D = 4608
FF = 36864
SEQ = 384
BLOCK = 128
BATCH = 64
OWN = D // 8
ROWS = D // 64
PIECE = ROWS + 8
CHUNKS = 3
SCALE = math.sqrt(FF * D / BATCH)
F32 = jnp.float32
MESH = pl.DeviceIdType.MESH


def ready_x(group):
    return lax.rem(3 * (group + 4), 5)


def group_of(x):
    return lax.rem(2 * x + 1, 5)


def kernel(
    h_hbm, g_ref, noise_ref, out_ref, mean_ref,
    h_ref, g_pair, win, a_half, gram_own, gram_in, s_in, x_out, x_own, x_in, sx_in, y_out, y_in,
    pair_recv, load_sem, send_sem, pair_sem, win_sem, gram_sem, s_sem, x_sem, sx_sem, y_sem,
):
    dp, t = lax.axis_index("dp"), lax.axis_index("tensor")
    zh, x, y = dp // 32, lax.rem(dp // 8, 4), lax.rem(dp, 8)
    zl, q = t // 2, lax.rem(t, 2)
    column = group_of(x)

    def device(zh_, x_, y_, zl_, q_):
        return (zh_ * 32 + x_ * 8 + y_, zl_ * 2 + q_)

    def peer_z(k):
        return device(zh, x, y, lax.rem(zl + k, 4), q)

    def peer_t(k):
        return (dp, lax.rem(t + k, 8))

    def peer_x(k):
        return device(zh, lax.rem(x + k, 4), y, zl, q)

    partner = (dp, t + 1 - 2 * q)
    sends = []

    def send(src, dst, recv, to):
        copy = pltpu.make_async_remote_copy(
            src_ref=src, dst_ref=dst, send_sem=send_sem.at[len(sends)], recv_sem=recv,
            device_id=to, device_id_type=MESH,
        )
        copy.start()
        sends.append(copy)

    def arrived(dst, recv):
        pltpu.make_async_copy(dst, dst, recv).wait()

    barrier = pltpu.get_barrier_semaphore()
    sources = [peer_t(k) for k in range(1, 8)] + [peer_x(k) for k in range(1, 4)]
    x_src = ready_x(zl)
    zl_src = zh * 2 + x // 2
    for k in range(16):
        sources.append(device(k // 8, x_src, k % 8, zl_src, q))
    for source in sources:
        pl.semaphore_signal(barrier, inc=1, device_id=source, device_id_type=MESH)

    part = h_ref.shape[1] // CHUNKS
    loads = []
    for c in range(CHUNKS):
        cut = pl.ds(c * part, part)
        loads.append(pltpu.make_async_copy(h_hbm.at[:, cut], h_ref.at[:, cut], load_sem.at[c]))
        loads[-1].start()
    loads[0].wait()
    win[zl] = h_ref[:, :BLOCK]
    pl.semaphore_wait(barrier, len(sources))

    send(g_ref, g_pair, pair_sem.at[0], partner)
    for k in range(1, 4):
        send(win.at[zl], win.at[zl], win_sem.at[zl], peer_z(k))

    gram = None
    for c in range(CHUNKS):
        if c:
            loads[c].wait()
        h = h_ref[:, c * part:(c + 1) * part]
        term = lax.dot_general(h, h, (((1,), (1,)), ((), ())), preferred_element_type=F32)
        gram = term if gram is None else gram + term
    blocks = [(0, 0), (0, 1), (0, 2), (1, 1), (1, 2), (2, 2)]

    def cut(matrix, b, p):
        i, j = blocks[b]
        return matrix[i * 128 + p * 32:i * 128 + (p + 1) * 32, j * 128:(j + 1) * 128]

    for b in range(6):
        for p in range(4):
            a_half[b // 3, p, b % 3] = cut(gram, b, p)
    send(a_half.at[1 - q], pair_recv, pair_sem.at[1], partner)

    arrived(g_pair, pair_sem.at[0])
    grad = None
    for ref in (g_ref, g_pair):
        g = ref[...]
        term = lax.dot_general(g, g, (((0,), (0,)), ((), ())), preferred_element_type=F32)
        grad = term if grad is None else grad + term
    for half in range(2):
        @pl.when(q == half)
        def _():
            for b in range(3):
                for p in range(4):
                    gram_own[p, 1, b] = cut(grad, half * 3 + b, p)

    arrived(pair_recv, pair_sem.at[1])
    gram_own[:, 0] = a_half[q] + pair_recv[...]
    for k in range(1, 4):
        to = lax.rem(zl + k, 4)
        send(gram_own.at[to], gram_in.at[k - 1], gram_sem.at[k - 1], peer_z(k))

    for k in range(1, 4):
        at = lax.rem(zl + k, 4)
        arrived(win.at[at], win_sem.at[at])
    for k in range(4):
        window = win[group_of(lax.rem(x + k, 4))]
        for side, ref in enumerate((g_ref, g_pair)):
            bucket = jnp.dot(ref[...], window, preferred_element_type=F32)
            if k:
                x_out[k - 1, side] = bucket
                send(x_out.at[k - 1, side], x_in.at[k - 1, side], x_sem.at[k - 1, side], peer_x(k))
            else:
                x_own[side] = bucket

    for k in range(1, 4):
        arrived(gram_in.at[k - 1], gram_sem.at[k - 1])
    total = gram_own[zl]
    for k in range(3):
        total = total + gram_in[k]
    both = total[0] * total[1]
    third = (2 - q).astype(F32)
    weighed = both[0] + 2.0 * both[1] + third * both[2]
    s_in[t] = jnp.full((8, 128), jnp.sum(weighed), F32)
    for k in range(1, 8):
        send(s_in.at[t], s_in.at[t], s_sem.at[t], peer_t(k))
    for k in range(1, 8):
        at = lax.rem(t + k, 8)
        arrived(s_in.at[at], s_sem.at[at])
    square = s_in[0]
    for k in range(1, 8):
        square = square + s_in[k]
    sx_in[x] = square
    for k in range(1, 4):
        send(sx_in.at[x], sx_in.at[x], sx_sem.at[x], peer_x(k))
    for k in range(1, 4):
        at = lax.rem(x + k, 4)
        arrived(sx_in.at[at], sx_sem.at[at])
    squares = sx_in[0] + sx_in[1] + sx_in[2] + sx_in[3]

    def factor(sq):
        return (1.0 / jnp.maximum(jnp.sqrt(sq), 1.0))[:1]

    own_factor = factor(sx_in[x])
    factors = [factor(sx_in[lax.rem(x + 4 - k, 4)]) for k in range(1, 4)]
    me = zh * 8 + y
    for side in range(2):
        for k in range(1, 4):
            arrived(x_in.at[k - 1, side], x_sem.at[k - 1, side])
        x_to = lax.rem(zl, 2) * 2 + (q if side == 0 else 1 - q)
        for r in range(8):
            rows = slice(r * ROWS, (r + 1) * ROWS)
            acc = own_factor * x_own[side, rows]
            for k in range(3):
                acc = acc + factors[k] * x_in[k, side, rows]
            y_out[side, r, :ROWS] = acc
            y_out[side, r, ROWS:] = squares
            send(y_out.at[side, r], y_in.at[me], y_sem.at[me], device(zl // 2, x_to, r, column, q))

    summed = None
    for k in range(16):
        arrived(y_in.at[k], y_sem.at[k])
        summed = y_in[k] if summed is None else summed + y_in[k]
    out_ref[...] = SCALE * summed[:ROWS] + noise_ref[...]
    mean_ref[...] = summed[ROWS:] / BATCH
    for copy in sends:
        copy.wait_send()


def shards(hidden_act, out_grad, privacy_noise):
    dma = pltpu.SemaphoreType.DMA
    vmem = pl.BlockSpec(memory_space=pltpu.VMEM)
    bf16 = jnp.bfloat16
    n_sends = 1 + 3 + 1 + 3 + 6 + 7 + 3 + 16
    update, mean = pl.pallas_call(
        kernel,
        out_shape=(jax.ShapeDtypeStruct((ROWS, BLOCK), F32), jax.ShapeDtypeStruct((8, 128), F32)),
        in_specs=[pl.BlockSpec(memory_space=pl.ANY), vmem, vmem],
        out_specs=(vmem, vmem),
        scratch_shapes=[
            pltpu.VMEM((SEQ, FF // 8), bf16),
            pltpu.VMEM((OWN, SEQ), bf16),
            pltpu.VMEM((4, SEQ, BLOCK), bf16),
            pltpu.VMEM((2, 4, 3, 32, 128), F32),
            pltpu.VMEM((4, 2, 3, 32, 128), F32),
            pltpu.VMEM((3, 2, 3, 32, 128), F32),
            pltpu.VMEM((8, 8, 128), F32),
            pltpu.VMEM((3, 2, OWN, BLOCK), F32),
            pltpu.VMEM((2, OWN, BLOCK), F32),
            pltpu.VMEM((3, 2, OWN, BLOCK), F32),
            pltpu.VMEM((4, 8, 128), F32),
            pltpu.VMEM((2, 8, PIECE, BLOCK), F32),
            pltpu.VMEM((16, PIECE, BLOCK), F32),
            pltpu.VMEM((4, 3, 32, 128), F32),
            dma((CHUNKS,)),
            dma((n_sends,)),
            dma((2,)),
            dma((4,)),
            dma((3,)),
            dma((8,)),
            dma((3, 2)),
            dma((4,)),
            dma((16,)),
        ],
        compiler_params=pltpu.CompilerParams(
            collective_id=0, has_side_effects=True, vmem_limit_bytes=40 * 2**20
        ),
        cost_estimate=pl.CostEstimate(flops=4 * 10**9, bytes_accessed=5 * 10**6, transcendentals=0),
    )(hidden_act, out_grad.T, privacy_noise)
    return (update, mean[0, 0])


def solution(mesh):
    return jax.shard_map(
        shards,
        mesh=mesh,
        in_specs=(P("dp", "tensor"), P("dp", "tensor"), P("dp", "tensor")),
        out_specs=(P("dp", "tensor"), P()),
        check_vma=False,
    )
```

```python
import math

import jax
import jax.numpy as jnp
from jax import lax
from jax.experimental import pallas as pl
from jax.experimental.pallas import tpu as pltpu
from jax.sharding import PartitionSpec as P

D = 4608
FF = 36864
SEQ = 384
BLOCK = 128
BATCH = 64
OWN = D // 8
ROWS = D // 64
PIECE = ROWS + 8
CODED = OWN + 16
SHARE = 2 * ROWS + 16
SPAN = 86.0
STRIP = 96
CHUNKS = 3
SCALE = math.sqrt(FF * D / BATCH)
F32 = jnp.float32
MESH = pl.DeviceIdType.MESH


def ready_x(group):
    return lax.rem(3 * (group + 4), 5)


def group_of(x):
    return lax.rem(2 * x + 1, 5)


def scale_of(top):
    return (top * 1.01).astype(jnp.bfloat16).astype(F32)


def encode(value, inverse):
    root = jnp.sqrt(jnp.minimum(jnp.abs(value) * inverse, 1.0))
    code = jnp.exp(root * (2 * SPAN) - SPAN)
    return jnp.where(value < 0, -code, code).astype(jnp.bfloat16)


def decode(code, scale):
    code = code.astype(F32)
    root = jnp.log(jnp.abs(code)) * (0.5 / SPAN) + 0.5
    value = root * root * scale
    return jnp.where(code < 0, -value, value)


def inverse_of(scale):
    return 1.0 / jnp.maximum(scale, 1e-30)


def kernel(
    h_hbm, g_hbm, noise_hbm, out_ref, mean_ref,
    h_ref, g_ref, noise_ref, g_pair, win, a_half, gram_own, pair_recv, gram_in, s_in, bucket_ref, x_out, x_in, sx_in,
    acc_ref, y_out, y_in, p_out, p_in,
    load_sem, send_sem, x_send, pair_sem, win_sem, gram_sem, s_sem, x_sem, sx_sem, y_sem, p_sem,
):
    dp, t = lax.axis_index("dp"), lax.axis_index("tensor")
    zh, x, y = dp // 32, lax.rem(dp // 8, 4), lax.rem(dp, 8)
    zl, q = t // 2, lax.rem(t, 2)
    column = group_of(x)

    def device(zh_, x_, y_, zl_, q_):
        return (zh_ * 32 + x_ * 8 + y_, zl_ * 2 + q_)

    def peer_z(k):
        return device(zh, x, y, lax.rem(zl + k, 4), q)

    def peer_t(k):
        return (dp, lax.rem(t + k, 8))

    def peer_x(k):
        return device(zh, lax.rem(x + k, 4), y, zl, q)

    def peer_y(k):
        return device(zh, x, lax.rem(y + k, 8), zl, q)

    partner = (dp, t + 1 - 2 * q)
    sends = []

    def remote(src, dst, sent, recv, to):
        return pltpu.make_async_remote_copy(
            src_ref=src, dst_ref=dst, send_sem=sent, recv_sem=recv, device_id=to, device_id_type=MESH
        )

    def send(src, dst, recv, to):
        sends.append(remote(src, dst, send_sem.at[len(sends)], recv, to))
        sends[-1].start()

    def arrived(dst, recv):
        pltpu.make_async_copy(dst, dst, recv).wait()

    barrier = pltpu.get_barrier_semaphore()
    sources = [peer_t(k) for k in range(1, 8)] + [peer_x(k) for k in range(1, 4)] + [peer_y(k) for k in range(1, 8)]
    for k in range(2):
        sources.append(device(k, ready_x(zl), y, zh * 2 + x // 2, q))
    for source in sources:
        pl.semaphore_signal(barrier, inc=1, device_id=source, device_id_type=MESH)

    part = h_ref.shape[1] // CHUNKS
    loads = []

    def load(src, dst):
        loads.append(pltpu.make_async_copy(src, dst, load_sem.at[len(loads)]))
        loads[-1].start()

    for c in range(CHUNKS):
        load(h_hbm.at[:, pl.ds(c * part, part)], h_ref.at[:, pl.ds(c * part, part)])
        if c == 0:
            load(g_hbm, g_ref)
    load(noise_hbm, noise_ref)
    loads[0].wait()
    win[zl] = h_ref[:, :BLOCK]
    loads[1].wait()
    pl.semaphore_wait(barrier, len(sources))

    send(g_ref, g_pair, pair_sem.at[0], partner)
    for k in range(1, 4):
        send(win.at[zl], win.at[zl], win_sem.at[zl], peer_z(k))

    def share(j, side):
        group = lax.rem(zl + j, 4)
        owner = ready_x(group)
        bucket = jnp.dot((g_ref, g_pair)[side][...], win[group], preferred_element_type=F32)
        bucket_ref[j, side] = bucket
        scale = scale_of(jnp.max(jnp.abs(bucket)))
        inverse = inverse_of(scale)
        for row in range(0, OWN, STRIP):
            rows = slice(row, row + STRIP)
            x_out[j, side, rows] = encode(bucket_ref[j, side, rows], inverse)
        x_out[j, side, OWN:] = jnp.full((16, BLOCK), scale, F32).astype(jnp.bfloat16)
        copy = remote(
            x_out.at[j, side], x_in.at[x, side], x_send.at[j, side], x_sem.at[x, side], device(zh, owner, y, zl, q)
        )

        @pl.when(owner != x)
        def _():
            copy.start()
        return owner, copy

    shares = [share(0, 0)]

    gram = None
    for c in range(CHUNKS):
        if c:
            loads[c + 1].wait()
        h = h_ref[:, c * part:(c + 1) * part]
        term = lax.dot_general(h, h, (((1,), (1,)), ((), ())), preferred_element_type=F32)
        gram = term if gram is None else gram + term
    blocks = [(0, 0), (0, 1), (0, 2), (1, 1), (1, 2), (2, 2)]

    def cut(matrix, b, p):
        i, j = blocks[b]
        return matrix[i * 128 + p * 32:i * 128 + (p + 1) * 32, j * 128:(j + 1) * 128]

    for b in range(6):
        for p in range(4):
            a_half[b // 3, p, b % 3] = cut(gram, b, p)
    send(a_half.at[1 - q], pair_recv, pair_sem.at[1], partner)

    arrived(g_pair, pair_sem.at[0])
    grad = None
    for ref in (g_ref, g_pair):
        g = ref[...]
        term = lax.dot_general(g, g, (((0,), (0,)), ((), ())), preferred_element_type=F32)
        grad = term if grad is None else grad + term
    for half in range(2):
        @pl.when(q == half)
        def _():
            for b in range(3):
                for p in range(4):
                    gram_own[p, 1, b] = cut(grad, half * 3 + b, p)

    arrived(pair_recv, pair_sem.at[1])
    gram_own[:, 0] = a_half[q] + pair_recv[...]
    for k in range(1, 4):
        to = lax.rem(zl + k, 4)
        send(gram_own.at[to], gram_in.at[k - 1], gram_sem.at[k - 1], peer_z(k))

    shares.append(share(0, 1))
    for k in range(1, 4):
        at = lax.rem(zl + k, 4)
        arrived(win.at[at], win_sem.at[at])
        shares += [share(k, 0), share(k, 1)]

    for k in range(1, 4):
        arrived(gram_in.at[k - 1], gram_sem.at[k - 1])
    total = gram_own[zl]
    for k in range(3):
        total = total + gram_in[k]
    both = total[0] * total[1]
    third = (2 - q).astype(F32)
    weighed = both[0] + 2.0 * both[1] + third * both[2]
    s_in[t] = jnp.full((8, 128), jnp.sum(weighed), F32)
    for k in range(1, 8):
        send(s_in.at[t], s_in.at[t], s_sem.at[t], peer_t(k))
    for k in range(1, 8):
        at = lax.rem(t + k, 8)
        arrived(s_in.at[at], s_sem.at[at])
    square = s_in[0]
    for k in range(1, 8):
        square = square + s_in[k]
    sx_in[x] = square
    for k in range(1, 4):
        send(sx_in.at[x], sx_in.at[x], sx_sem.at[x], peer_x(k))
    for k in range(1, 4):
        at = lax.rem(x + k, 4)
        arrived(sx_in.at[at], sx_sem.at[at])
    squares = sx_in[0] + sx_in[1] + sx_in[2] + sx_in[3]

    def factor(sq):
        return (1.0 / jnp.maximum(jnp.sqrt(sq), 1.0))[:1]

    own = lax.rem(column - zl + 4, 4)
    own_factor = factor(sx_in[x])
    others = [lax.rem(x + k, 4) for k in range(1, 4)]
    factors = [factor(sx_in[at]) for at in others]
    for side in range(2):
        for at in others:
            arrived(x_in.at[at, side], x_sem.at[at, side])
        scales = [f * x_in[at, side, OWN:][:1].astype(F32) for f, at in zip(factors, others)]
        for row in range(0, OWN, STRIP):
            rows = slice(row, row + STRIP)
            acc = own_factor * bucket_ref[own, side, rows]
            for scale, at in zip(scales, others):
                acc = acc + decode(x_in[at, side, rows], scale)
            acc_ref[side, rows] = acc

    high = squares.astype(jnp.bfloat16).astype(F32)
    middle = (squares - high).astype(jnp.bfloat16).astype(F32)
    low = squares - high - middle
    line = lax.broadcasted_iota(jnp.int32, (8, 128), 0)
    top = jnp.max(jnp.abs(acc_ref[...]), axis=(0, 1))
    scale = scale_of(jnp.max(top))
    inverse = inverse_of(scale)
    head = jnp.where(line == 0, scale, jnp.where(line == 1, high, jnp.where(line == 2, middle, low)))
    tile = jnp.concatenate([head, head], axis=0).astype(jnp.bfloat16)
    for k in range(1, 8):
        to = lax.rem(y + k, 8)
        rows = pl.ds(pl.multiple_of(to * ROWS, 8), ROWS)
        both = jnp.concatenate([acc_ref[0, rows], acc_ref[1, rows]], axis=0)
        y_out[k - 1, :2 * ROWS] = encode(both, inverse)
        y_out[k - 1, 2 * ROWS:] = tile
        send(y_out.at[k - 1], y_in.at[y], y_sem.at[y], peer_y(k))
    rows = pl.ds(pl.multiple_of(y * ROWS, 8), ROWS)
    acc = jnp.concatenate([acc_ref[0, rows], acc_ref[1, rows]], axis=0)
    y_in[y, 2 * ROWS:] = tile
    for k in range(1, 8):
        at = lax.rem(y + k, 8)
        arrived(y_in.at[at], y_sem.at[at])
        scale = y_in[at, 2 * ROWS:].astype(F32)[:1]
        acc = acc + decode(y_in[at, :2 * ROWS], scale)
    squares = None
    for k in range(8):
        head = y_in[k, 2 * ROWS:].astype(F32)
        one = head[1:2] + head[2:3] + head[3:4]
        squares = one if squares is None else squares + one

    for side in range(2):
        x_to = lax.rem(zl, 2) * 2 + (q if side == 0 else 1 - q)
        p_out[side, :ROWS] = acc[side * ROWS:(side + 1) * ROWS]
        p_out[side, ROWS:] = jnp.broadcast_to(squares, (8, 128))
        send(p_out.at[side], p_in.at[zh], p_sem.at[zh], device(zl // 2, x_to, y, column, q))
    for k in range(2):
        arrived(p_in.at[k], p_sem.at[k])
    loads[-1].wait()
    summed = p_in[0] + p_in[1]
    out_ref[...] = SCALE * summed[:ROWS] + noise_ref[...]
    mean_ref[...] = summed[ROWS:ROWS + 1, :1] / BATCH
    for copy in sends:
        copy.wait_send()
    for owner, copy in shares:
        @pl.when(owner != x)
        def _():
            copy.wait_send()


def shards(hidden_act, out_grad, privacy_noise):
    dma = pltpu.SemaphoreType.DMA
    hbm = pl.BlockSpec(memory_space=pl.ANY)
    vmem = pl.BlockSpec(memory_space=pltpu.VMEM)
    bf16 = jnp.bfloat16
    n_sends = 1 + 3 + 1 + 3 + 7 + 3 + 7 + 2
    update, mean = pl.pallas_call(
        kernel,
        out_shape=(pltpu.VMEM((ROWS, BLOCK), F32), pltpu.VMEM((1, 1), F32)),
        in_specs=[hbm, hbm, hbm],
        out_specs=(vmem, vmem),
        scratch_shapes=[
            pltpu.VMEM((SEQ, FF // 8), bf16),
            pltpu.VMEM((OWN, SEQ), bf16),
            pltpu.VMEM((ROWS, BLOCK), F32),
            pltpu.VMEM((OWN, SEQ), bf16),
            pltpu.VMEM((4, SEQ, BLOCK), bf16),
            pltpu.VMEM((2, 4, 3, 32, 128), F32),
            pltpu.VMEM((4, 2, 3, 32, 128), F32),
            pltpu.VMEM((4, 3, 32, 128), F32),
            pltpu.VMEM((3, 2, 3, 32, 128), F32),
            pltpu.VMEM((8, 8, 128), F32),
            pltpu.VMEM((4, 2, OWN, BLOCK), F32),
            pltpu.VMEM((4, 2, CODED, BLOCK), bf16),
            pltpu.VMEM((4, 2, CODED, BLOCK), bf16),
            pltpu.VMEM((4, 8, 128), F32),
            pltpu.VMEM((2, OWN, BLOCK), F32),
            pltpu.VMEM((7, SHARE, BLOCK), bf16),
            pltpu.VMEM((8, SHARE, BLOCK), bf16),
            pltpu.VMEM((2, PIECE, BLOCK), F32),
            pltpu.VMEM((2, PIECE, BLOCK), F32),
            dma((CHUNKS + 2,)),
            dma((n_sends,)),
            dma((4, 2)),
            dma((2,)),
            dma((4,)),
            dma((3,)),
            dma((8,)),
            dma((4, 2)),
            dma((4,)),
            dma((8,)),
            dma((2,)),
        ],
        compiler_params=pltpu.CompilerParams(
            collective_id=0, has_side_effects=True, vmem_limit_bytes=60 * 2**20
        ),
        cost_estimate=pl.CostEstimate(flops=4 * 10**9, bytes_accessed=5 * 10**6, transcendentals=0),
    )(hidden_act, out_grad.T, privacy_noise)
    return (update, mean.reshape(()))


def solution(mesh):
    return jax.shard_map(
        shards,
        mesh=mesh,
        in_specs=(P("dp", "tensor"), P("dp", "tensor"), P("dp", "tensor")),
        out_specs=(P("dp", "tensor"), P()),
        check_vma=False,
    )
```

```python
import math

import jax
import jax.numpy as jnp
from jax import lax
from jax.experimental import pallas as pl
from jax.experimental.pallas import tpu as pltpu
from jax.sharding import PartitionSpec as P

D = 4608
FF = 36864
SEQ = 384
BLOCK = 128
BATCH = 64
OWN = D // 8
ROWS = D // 64
PIECE = ROWS + 8
PAIR = 2 * ROWS
CODED = PAIR + 16
GRAM = 2 * 3 * 32
SPAN = 86.0
CHUNKS = 3
SCALE = math.sqrt(FF * D / BATCH)
F32 = jnp.float32
MESH = pl.DeviceIdType.MESH


def turn_of(group):
    return lax.rem(3 * (group + 4), 5)


def group_at(turn):
    return lax.rem(2 * turn + 1, 5)


def scale_of(value):
    top = jnp.max(jnp.max(jnp.abs(value), axis=0, keepdims=True), axis=1, keepdims=True)
    return (top * 1.01).astype(jnp.bfloat16).astype(F32)


def encode(value, inverse):
    root = jnp.sqrt(jnp.minimum(jnp.abs(value) * inverse, 1.0))
    code = jnp.exp(root * (2 * SPAN) - SPAN)
    return jnp.where(value < 0, -code, code)


def decode(code, scale):
    code = code.astype(F32)
    root = jnp.log(jnp.abs(code)) * (0.5 / SPAN) + 0.5
    value = root * root * scale
    return jnp.where(code < 0, -value, value)


def inverse_of(scale):
    return 1.0 / jnp.maximum(scale, 1e-30)


def pack(value, exact):
    scale = scale_of(value)
    high = exact.astype(jnp.bfloat16).astype(F32)
    middle = (exact - high).astype(jnp.bfloat16).astype(F32)
    low = exact - high - middle
    line = lax.broadcasted_iota(jnp.int32, (8, BLOCK), 0)
    head = jnp.where(line == 0, scale, jnp.where(line == 1, high, jnp.where(line == 2, middle, low)))
    return jnp.concatenate([encode(value, inverse_of(scale)), head], axis=0).astype(jnp.bfloat16)


def unpack(packed):
    packed = packed.astype(F32)
    rows = packed.shape[0] - 8
    head = packed[rows:]
    return decode(packed[:rows], head[:1]), head[1:2] + head[2:3] + head[3:4]


def kernel(
    h_hbm, g_hbm, noise_hbm, out_ref, mean_ref,
    h_ref, g_ref, noise_ref, g_pair, win, a_half, gram_own, pair_recv, gram_out, gram_in, s_in, bucket_ref, x_out, x_in,
    x_value, sx_in, s_line, acc_ref, y_out, y_in, p_out, p_in,
    load_sem, send_sem, x_send, p_send, pass_send, pair_sem, win_sem, gram_sem, s_sem, x_sem, sx_sem, y_sem, p_sem,
):
    dp, t = lax.axis_index("dp"), lax.axis_index("tensor")
    zh, x, y = dp // 32, lax.rem(dp // 8, 4), lax.rem(dp, 8)
    zl, q = t // 2, lax.rem(t, 2)
    column = group_at(lax.rem(x + 8 - y, 4))

    def device(zh_, x_, y_, zl_, q_):
        return (zh_ * 32 + x_ * 8 + y_, zl_ * 2 + q_)

    def peer_z(k):
        return device(zh, x, y, lax.rem(zl + k, 4), q)

    def peer_t(k):
        return (dp, lax.rem(t + k, 8))

    def peer_x(k):
        return device(zh, lax.rem(x + k, 4), y, zl, q)

    def peer_y(k):
        return device(zh, x, lax.rem(y + k, 8), zl, q)

    partner = (dp, t + 1 - 2 * q)
    sends = []

    def remote(src, dst, sent, recv, to):
        return pltpu.make_async_remote_copy(
            src_ref=src, dst_ref=dst, send_sem=sent, recv_sem=recv, device_id=to, device_id_type=MESH
        )

    def send(src, dst, recv, to):
        sends.append(remote(src, dst, send_sem.at[len(sends)], recv, to))
        sends[-1].start()

    def arrived(dst, recv):
        pltpu.make_async_copy(dst, dst, recv).wait()

    barrier = pltpu.get_barrier_semaphore()
    def greet(to):
        pl.semaphore_signal(barrier, inc=1, device_id=to, device_id_type=MESH)

    source_x, source_z = lax.rem(turn_of(zl) + y, 4), zh * 2 + x // 2
    for k in range(2):
        pl.when(~((k == zh) & (source_x == x) & (source_z == zl)))(lambda k=k: greet(device(k, source_x, y, source_z, q)))
    for to in [peer_y(k) for k in range(1, 8)] + [peer_t(k) for k in range(1, 8)] + [peer_x(k) for k in range(1, 4)]:
        greet(to)
    own_x = [lax.rem(zl, 2) * 2 + (q if side == 0 else 1 - q) for side in range(2)]
    stays = [(own_x[side] == x) & (zl // 2 == zh) & (column == zl) for side in range(2)]
    greeted = 17 + sum(1 - stay.astype(jnp.int32) for stay in stays)

    part = h_ref.shape[1] // CHUNKS
    loads = []

    def load(src, dst):
        loads.append(pltpu.make_async_copy(src, dst, load_sem.at[len(loads)]))
        loads[-1].start()

    for c in range(CHUNKS):
        load(h_hbm.at[:, pl.ds(c * part, part)], h_ref.at[:, pl.ds(c * part, part)])
        if c == 0:
            load(g_hbm, g_ref)
    load(noise_hbm, noise_ref)
    def grams(left, right, axis):
        def product(a, b):
            return lax.dot_general(a, b, (((axis,), (axis,)), ((), ())), preferred_element_type=F32)
        return product(left, right(slice(0, 256))), product(right(slice(256, 384)), right(slice(256, 384)))

    def act_term(c):
        columns = slice(c * part, (c + 1) * part)
        return grams(h_ref[:, columns], lambda rows: h_ref[rows, columns], 1)

    def plus(a, b):
        return tuple(i + j for i, j in zip(a, b))

    loads[0].wait()
    win[zl] = h_ref[:, :BLOCK]
    gram = act_term(0)
    for c in range(1, CHUNKS):
        loads[c + 1].wait()
        gram = plus(gram, act_term(c))
    loads[1].wait()
    blocks = [(0, 0), (1, 0), (2, 0), (1, 1), (2, 1), (2, 2)]

    def cut(matrices, b, p):
        i, j = blocks[b]
        if b == 5:
            return matrices[1][p * 32:(p + 1) * 32]
        return matrices[0][i * 128 + p * 32:i * 128 + (p + 1) * 32, j * 128:(j + 1) * 128]

    for b in range(6):
        for p in range(4):
            a_half[b // 3, p, b % 3] = cut(gram, b, p)
    pl.semaphore_wait(barrier, greeted)
    low = (zl < 2).astype(jnp.int32)
    near = [zl + 1 - 2 * lax.rem(zl, 2), 1 + low, 3 * low]

    def send_window(to):
        send(win.at[zl], win.at[zl], win_sem.at[zl], device(zh, x, y, to, q))

    middle = (zl == 1) | (zl == 2)
    send_window(near[0])
    send_window(near[1])

    def pass_window(of, to, n):
        copy = remote(win.at[of], win.at[of], pass_send.at[n], win_sem.at[of], device(zh, x, y, to, q))
        pl.when(middle)(copy.start)
        shares.append((middle, copy))

    shares = []
    pass_window(zl, near[2], 0)
    send(g_ref, g_pair, pair_sem.at[0], partner)
    send(a_half.at[1 - q], pair_recv, pair_sem.at[1], partner)

    def share(slot, side, group):
        bucket = jnp.dot((g_ref, g_pair)[side][...], win[group], preferred_element_type=F32)
        scale = scale_of(bucket)
        inverse = inverse_of(scale)
        tile = jnp.broadcast_to(scale, (16, BLOCK)).astype(jnp.bfloat16)
        for b in range(4):
            rows = slice(b * ROWS, (b + 1) * ROWS), slice((b + 4) * ROWS, (b + 5) * ROWS)
            value = jnp.concatenate([bucket[r] for r in rows], axis=0)
            bucket_ref[group, side, b] = value
            x_out[slot, side, b, :PAIR] = encode(value, inverse).astype(jnp.bfloat16)
            x_out[slot, side, b, PAIR:] = tile
        for k in (1, 3, 2):
            to = lax.rem(x + k, 4)
            b = lax.rem(to + 4 - turn_of(group), 4)
            copy = remote(
                x_out.at[slot, side, b], x_in.at[x, side, b], x_send.at[slot, side, k - 1], x_sem.at[x, side, b],
                device(zh, to, y, zl, q),
            )
            copy.start()
            shares.append((None, copy))

    arrived(g_pair, pair_sem.at[0])
    grad = plus(*(grams(ref[...], lambda rows: ref[:, rows], 0) for ref in (g_ref, g_pair)))
    for half in range(2):
        @pl.when(q == half)
        def _():
            for b in range(3):
                for p in range(4):
                    gram_own[p, 1, b] = cut(grad, half * 3 + b, p)
    share(0, 0, zl)

    arrived(pair_recv, pair_sem.at[1])
    gram_own[:, 0] = a_half[q] + pair_recv[...]
    tops = [scale_of(gram_own[:, i].reshape(4 * GRAM // 2, 128)) for i in range(2)]
    for k in range(1, 4):
        to = lax.rem(zl + k, 4)
        for i, top in enumerate(tops):
            code = encode(gram_own[to, i].reshape(GRAM // 2, 128), inverse_of(top))
            gram_out[k - 1, i * GRAM // 2:(i + 1) * GRAM // 2] = code.astype(jnp.bfloat16)
        line = lax.broadcasted_iota(jnp.int32, (16, 128), 0)
        gram_out[k - 1, GRAM:] = jnp.where(line < 8, tops[0], tops[1]).astype(jnp.bfloat16)
        send(gram_out.at[k - 1], gram_in.at[k - 1], gram_sem.at[k - 1], peer_z(k))

    share(0, 1, zl)

    def share_near(n):
        arrived(win.at[near[n]], win_sem.at[near[n]])
        if n == 2:
            pass_window(near[2], near[0], 1)
        for side in range(2):
            share(n + 1, side, near[n])

    share_near(0)
    share_near(1)
    share_near(2)

    for k in range(1, 4):
        arrived(gram_in.at[k - 1], gram_sem.at[k - 1])
    total = [gram_own[zl, i] for i in range(2)]
    for k in range(3):
        got = gram_in[k].astype(F32)
        for i in range(2):
            value = decode(got[i * GRAM // 2:(i + 1) * GRAM // 2], got[GRAM + 8 * i:GRAM + 8 * i + 1])
            total[i] = total[i] + value.reshape(3, 32, 128)
    both = total[0] * total[1]
    third = (2 - q).astype(F32)
    weighed = both[0] + 2.0 * both[1] + third * both[2]
    s_in[t] = jnp.full((8, 128), jnp.sum(weighed), F32)
    for k in range(1, 8):
        send(s_in.at[t], s_in.at[t], s_sem.at[t], peer_t(k))
    for k in range(1, 8):
        at = lax.rem(t + k, 8)
        arrived(s_in.at[at], s_sem.at[at])
    square = s_in[0]
    for k in range(1, 8):
        square = square + s_in[k]
    sx_in[x] = square
    for k in range(1, 4):
        send(sx_in.at[x], sx_in.at[x], sx_sem.at[x], peer_x(k))

    others = [lax.rem(x + k, 4) for k in range(1, 4)]

    def open_side(side):
        for k, at in enumerate(others):
            for b in range(4):
                arrived(x_in.at[at, side, b], x_sem.at[at, side, b])
                code = x_in[at, side, b].astype(F32)
                x_value[side, k, b] = decode(code[:PAIR], code[PAIR:PAIR + 1])

    def factor(sq):
        return (1.0 / jnp.maximum(jnp.sqrt(sq), 1.0))[:1]

    def add_side(side):
        for b in range(4):
            acc = own_factor * bucket_ref[group_at(lax.rem(x + 4 - b, 4)), side, b]
            for k in range(3):
                acc = acc + factors[k] * x_value[side, k, b]
            acc_ref[side, b * ROWS:(b + 1) * ROWS] = acc[:ROWS]
            acc_ref[side, (b + 4) * ROWS:(b + 5) * ROWS] = acc[ROWS:]
        for k in range(1, 8):
            rows = pl.ds(pl.multiple_of(lax.rem(y + k, 8) * ROWS, 8), ROWS)
            y_out[side, k - 1] = pack(acc_ref[side, rows], squares)
            send(y_out.at[side, k - 1], y_in.at[side, y], y_sem.at[side, y], peer_y(k))

    def to_owner(side):
        acc = acc_ref[side, pl.ds(pl.multiple_of(y * ROWS, 8), ROWS)]
        s_line[y] = jnp.broadcast_to(squares, (8, BLOCK))
        for k in range(1, 8):
            at = lax.rem(y + k, 8)
            arrived(y_in.at[side, at], y_sem.at[side, at])
            value, line = unpack(y_in[side, at])
            acc = acc + value
            s_line[at] = jnp.broadcast_to(line, (8, BLOCK))
        line = s_line[0]
        for k in range(1, 8):
            line = line + s_line[k]
        p_out[side] = pack(acc, line[:1])
        copy = remote(
            p_out.at[side], p_in.at[zh], p_send.at[side], p_sem.at[zh], device(zl // 2, own_x[side], y, column, q)
        )
        stay = pltpu.make_async_copy(p_out.at[side], p_in.at[zh], p_sem.at[zh])
        pl.when(stays[side])(stay.start)
        pl.when(~stays[side])(copy.start)
        shares.append((~stays[side], copy))

    open_side(0)
    for at in others:
        arrived(sx_in.at[at], sx_sem.at[at])
    squares = (sx_in[0] + sx_in[1] + sx_in[2] + sx_in[3])[:1]
    own_factor = factor(sx_in[x])
    factors = [factor(sx_in[at]) for at in others]
    add_side(0)
    open_side(1)
    add_side(1)
    to_owner(0)
    to_owner(1)
    summed = None
    for k in range(2):
        arrived(p_in.at[k], p_sem.at[k])
        got = unpack(p_in[k])
        summed = got if summed is None else plus(summed, got)
    loads[-1].wait()
    out_ref[...] = SCALE * summed[0] + noise_ref[...]
    mean_ref[...] = jnp.broadcast_to(summed[1] / BATCH, (8, BLOCK))
    for copy in sends:
        copy.wait_send()
    for wanted, copy in shares:
        if wanted is None:
            copy.wait_send()
        else:
            pl.when(wanted)(copy.wait_send)


def shards(hidden_act, out_grad, privacy_noise):
    dma = pltpu.SemaphoreType.DMA
    hbm = pl.BlockSpec(memory_space=pl.ANY)
    vmem = pl.BlockSpec(memory_space=pltpu.VMEM)
    bf16 = jnp.bfloat16
    n_sends = 1 + 2 + 1 + 3 + 7 + 3 + 14
    update, mean = pl.pallas_call(
        kernel,
        out_shape=(pltpu.VMEM((ROWS, BLOCK), F32), pltpu.VMEM((8, BLOCK), F32)),
        in_specs=[hbm, hbm, hbm],
        out_specs=(vmem, vmem),
        scratch_shapes=[
            pltpu.VMEM((SEQ, FF // 8), bf16),
            pltpu.VMEM((OWN, SEQ), bf16),
            pltpu.VMEM((ROWS, BLOCK), F32),
            pltpu.VMEM((OWN, SEQ), bf16),
            pltpu.VMEM((4, SEQ, BLOCK), bf16),
            pltpu.VMEM((2, 4, 3, 32, 128), F32),
            pltpu.VMEM((4, 2, 3, 32, 128), F32),
            pltpu.VMEM((4, 3, 32, 128), F32),
            pltpu.VMEM((3, GRAM + 16, 128), bf16),
            pltpu.VMEM((3, GRAM + 16, 128), bf16),
            pltpu.VMEM((8, 8, 128), F32),
            pltpu.VMEM((4, 2, 4, PAIR, BLOCK), F32),
            pltpu.VMEM((4, 2, 4, CODED, BLOCK), bf16),
            pltpu.VMEM((4, 2, 4, CODED, BLOCK), bf16),
            pltpu.VMEM((2, 3, 4, PAIR, BLOCK), F32),
            pltpu.VMEM((4, 8, 128), F32),
            pltpu.VMEM((8, 8, 128), F32),
            pltpu.VMEM((2, OWN, BLOCK), F32),
            pltpu.VMEM((2, 7, PIECE, BLOCK), bf16),
            pltpu.VMEM((2, 8, PIECE, BLOCK), bf16),
            pltpu.VMEM((2, PIECE, BLOCK), bf16),
            pltpu.VMEM((2, PIECE, BLOCK), bf16),
            dma((CHUNKS + 2,)),
            dma((n_sends,)),
            dma((4, 2, 4)),
            dma((2,)),
            dma((2,)),
            dma((2,)),
            dma((4,)),
            dma((3,)),
            dma((8,)),
            dma((4, 2, 4)),
            dma((4,)),
            dma((2, 8)),
            dma((2,)),
        ],
        compiler_params=pltpu.CompilerParams(
            collective_id=0, has_side_effects=True, vmem_limit_bytes=60 * 2**20
        ),
        cost_estimate=pl.CostEstimate(flops=4 * 10**9, bytes_accessed=5 * 10**6, transcendentals=0),
    )(hidden_act, out_grad.T, privacy_noise)
    return (update, mean[0, 0])


def solution(mesh):
    return jax.shard_map(
        shards,
        mesh=mesh,
        in_specs=(P("dp", "tensor"), P("dp", "tensor"), P("dp", "tensor")),
        out_specs=(P("dp", "tensor"), P()),
        check_vma=False,
    )
```

```python
import math

import jax
import jax.numpy as jnp
from jax import lax
from jax.experimental import pallas as pl
from jax.experimental.pallas import tpu as pltpu
from jax.sharding import PartitionSpec as P

D = 4608
FF = 36864
SEQ = 384
BLOCK = 128
BATCH = 64
OWN = D // 8
ROWS = D // 64
PIECE = ROWS + 8
PAIR = 2 * ROWS
CODED = PAIR + 16
GRAM = 2 * 3 * 32
SPAN = 86.0
CHUNKS = 3
SCALE = math.sqrt(FF * D / BATCH)
F32 = jnp.float32
MESH = pl.DeviceIdType.MESH


def turn_of(group):
    return lax.rem(3 * (group + 4), 5)


def group_at(turn):
    return lax.rem(2 * turn + 1, 5)


def scale_of(value):
    top = jnp.max(jnp.max(jnp.abs(value), axis=0, keepdims=True), axis=1, keepdims=True)
    return (top * 1.01).astype(jnp.bfloat16).astype(F32)


def encode(value, inverse):
    root = jnp.sqrt(jnp.minimum(jnp.abs(value) * inverse, 1.0))
    code = jnp.exp(root * (2 * SPAN) - SPAN)
    return jnp.where(value < 0, -code, code)


def decode(code, scale):
    code = code.astype(F32)
    root = jnp.log(jnp.abs(code)) * (0.5 / SPAN) + 0.5
    value = root * root * scale
    return jnp.where(code < 0, -value, value)


def inverse_of(scale):
    return 1.0 / jnp.maximum(scale, 1e-30)


def pack(value, exact):
    scale = scale_of(value)
    high = exact.astype(jnp.bfloat16).astype(F32)
    middle = (exact - high).astype(jnp.bfloat16).astype(F32)
    low = exact - high - middle
    line = lax.broadcasted_iota(jnp.int32, (8, BLOCK), 0)
    head = jnp.where(line == 0, scale, jnp.where(line == 1, high, jnp.where(line == 2, middle, low)))
    return jnp.concatenate([encode(value, inverse_of(scale)), head], axis=0).astype(jnp.bfloat16)


def unpack(packed):
    packed = packed.astype(F32)
    rows = packed.shape[0] - 8
    head = packed[rows:]
    return decode(packed[:rows], head[:1]), head[1:2] + head[2:3] + head[3:4]


def kernel(
    h_hbm, g_hbm, noise_hbm, out_ref, mean_ref,
    h_ref, g_ref, noise_ref, g_pair, win, a_half, gram_own, pair_recv, gram_out, gram_in, s_in, bucket_ref, x_out, x_in,
    x_value, sx_in, s_line, acc_ref, y_out, y_in, p_out, p_in,
    load_sem, send_sem, x_send, p_send, pass_send, pair_sem, win_sem, gram_sem, s_sem, x_sem, sx_sem, y_sem, p_sem,
):
    dp, t = lax.axis_index("dp"), lax.axis_index("tensor")
    zh, x, y = dp // 32, lax.rem(dp // 8, 4), lax.rem(dp, 8)
    zl, q = t // 2, lax.rem(t, 2)
    column = group_at(lax.rem(x + 8 - y, 4))

    def device(zh_, x_, y_, zl_, q_):
        return (zh_ * 32 + x_ * 8 + y_, zl_ * 2 + q_)

    def peer_z(k):
        return device(zh, x, y, lax.rem(zl + k, 4), q)

    def peer_t(k):
        return (dp, lax.rem(t + k, 8))

    def peer_x(k):
        return device(zh, lax.rem(x + k, 4), y, zl, q)

    def peer_y(k):
        return device(zh, x, lax.rem(y + k, 8), zl, q)

    partner = (dp, t + 1 - 2 * q)
    sends = []

    def remote(src, dst, sent, recv, to):
        return pltpu.make_async_remote_copy(
            src_ref=src, dst_ref=dst, send_sem=sent, recv_sem=recv, device_id=to, device_id_type=MESH
        )

    def send(src, dst, recv, to):
        sends.append(remote(src, dst, send_sem.at[len(sends)], recv, to))
        sends[-1].start()

    def arrived(dst, recv):
        pltpu.make_async_copy(dst, dst, recv).wait()

    barrier = pltpu.get_barrier_semaphore()
    def greet(to):
        pl.semaphore_signal(barrier, inc=1, device_id=to, device_id_type=MESH)

    source_x, source_z = lax.rem(turn_of(zl) + y, 4), zh * 2 + x // 2
    for k in range(2):
        pl.when(~((k == zh) & (source_x == x) & (source_z == zl)))(lambda k=k: greet(device(k, source_x, y, source_z, q)))
    for to in [peer_y(k) for k in range(1, 8)] + [peer_t(k) for k in range(1, 8)] + [peer_x(k) for k in range(1, 4)]:
        greet(to)
    own_x = [lax.rem(zl, 2) * 2 + (q if side == 0 else 1 - q) for side in range(2)]
    stays = [(own_x[side] == x) & (zl // 2 == zh) & (column == zl) for side in range(2)]
    greeted = 17 + sum(1 - stay.astype(jnp.int32) for stay in stays)

    part = h_ref.shape[1] // CHUNKS
    loads = []

    def load(src, dst):
        loads.append(pltpu.make_async_copy(src, dst, load_sem.at[len(loads)]))
        loads[-1].start()

    for c in range(CHUNKS):
        load(h_hbm.at[:, pl.ds(c * part, part)], h_ref.at[:, pl.ds(c * part, part)])
        if c == 0:
            load(g_hbm, g_ref)
    load(noise_hbm, noise_ref)
    def grams(left, right, axis):
        def product(a, b):
            return lax.dot_general(a, b, (((axis,), (axis,)), ((), ())), preferred_element_type=F32)
        return product(left, right(slice(0, 256))), product(right(slice(256, 384)), right(slice(256, 384)))

    def act_term(c):
        columns = slice(c * part, (c + 1) * part)
        return grams(h_ref[:, columns], lambda rows: h_ref[rows, columns], 1)

    def plus(a, b):
        return tuple(i + j for i, j in zip(a, b))

    loads[0].wait()
    win[zl] = h_ref[:, :BLOCK]
    gram = act_term(0)
    for c in range(1, CHUNKS):
        loads[c + 1].wait()
        gram = plus(gram, act_term(c))
    loads[1].wait()
    grad = grams(g_ref[...], lambda rows: g_ref[:, rows], 0)
    blocks = [(0, 0), (1, 0), (2, 0), (1, 1), (2, 1), (2, 2)]

    def cut(matrices, b, p):
        i, j = blocks[b]
        if b == 5:
            return matrices[1][p * 32:(p + 1) * 32]
        return matrices[0][i * 128 + p * 32:i * 128 + (p + 1) * 32, j * 128:(j + 1) * 128]

    for b in range(6):
        for p in range(4):
            a_half[b // 3, p, 0, b % 3] = cut(gram, b, p)
            a_half[b // 3, p, 1, b % 3] = cut(grad, b, p)
    pl.semaphore_wait(barrier, greeted)
    low = (zl < 2).astype(jnp.int32)
    near = [zl + 1 - 2 * lax.rem(zl, 2), 1 + low, 3 * low]

    def send_window(to):
        send(win.at[zl], win.at[zl], win_sem.at[zl], device(zh, x, y, to, q))

    middle = (zl == 1) | (zl == 2)
    send_window(near[0])
    send_window(near[1])

    def pass_window(of, to, n):
        copy = remote(win.at[of], win.at[of], pass_send.at[n], win_sem.at[of], device(zh, x, y, to, q))
        pl.when(middle)(copy.start)
        shares.append((middle, copy))

    shares = []
    pass_window(zl, near[2], 0)
    send(a_half.at[1 - q], pair_recv, pair_sem.at[1], partner)
    send(g_ref, g_pair, pair_sem.at[0], partner)

    def share(slot, side, group):
        bucket = jnp.dot((g_ref, g_pair)[side][...], win[group], preferred_element_type=F32)
        scale = scale_of(bucket)
        inverse = inverse_of(scale)
        tile = jnp.broadcast_to(scale, (16, BLOCK)).astype(jnp.bfloat16)
        for b in range(4):
            rows = slice(b * ROWS, (b + 1) * ROWS), slice((b + 4) * ROWS, (b + 5) * ROWS)
            value = jnp.concatenate([bucket[r] for r in rows], axis=0)
            bucket_ref[group, side, b] = value
            x_out[slot, side, b, :PAIR] = encode(value, inverse).astype(jnp.bfloat16)
            x_out[slot, side, b, PAIR:] = tile
        for k in (1, 3, 2):
            to = lax.rem(x + k, 4)
            b = lax.rem(to + 4 - turn_of(group), 4)
            copy = remote(
                x_out.at[slot, side, b], x_in.at[x, side, b], x_send.at[slot, side, k - 1], x_sem.at[x, side, b],
                device(zh, to, y, zl, q),
            )
            copy.start()
            shares.append((None, copy))

    share(0, 0, zl)
    arrived(pair_recv, pair_sem.at[1])
    gram_own[...] = a_half[q] + pair_recv[...]
    tops = [scale_of(gram_own[:, i].reshape(4 * GRAM // 2, 128)) for i in range(2)]
    for k in range(1, 4):
        to = lax.rem(zl + k, 4)
        for i, top in enumerate(tops):
            code = encode(gram_own[to, i].reshape(GRAM // 2, 128), inverse_of(top))
            gram_out[k - 1, i * GRAM // 2:(i + 1) * GRAM // 2] = code.astype(jnp.bfloat16)
        line = lax.broadcasted_iota(jnp.int32, (16, 128), 0)
        gram_out[k - 1, GRAM:] = jnp.where(line < 8, tops[0], tops[1]).astype(jnp.bfloat16)
        send(gram_out.at[k - 1], gram_in.at[k - 1], gram_sem.at[k - 1], peer_z(k))

    arrived(g_pair, pair_sem.at[0])
    share(0, 1, zl)

    def window_arrived(n):
        arrived(win.at[near[n]], win_sem.at[near[n]])

    def share_near(n):
        for side in range(2):
            share(n + 1, side, near[n])

    window_arrived(0)
    share_near(0)
    window_arrived(1)
    share_near(1)
    pl.when(middle)(lambda: window_arrived(2))
    pass_window(near[2], near[0], 1)

    for k in range(1, 4):
        arrived(gram_in.at[k - 1], gram_sem.at[k - 1])
    total = [gram_own[zl, i] for i in range(2)]
    for k in range(3):
        got = gram_in[k].astype(F32)
        for i in range(2):
            value = decode(got[i * GRAM // 2:(i + 1) * GRAM // 2], got[GRAM + 8 * i:GRAM + 8 * i + 1])
            total[i] = total[i] + value.reshape(3, 32, 128)
    both = total[0] * total[1]
    third = (2 - q).astype(F32)
    weighed = both[0] + 2.0 * both[1] + third * both[2]
    s_in[t] = jnp.full((8, 128), jnp.sum(weighed), F32)
    for k in range(1, 8):
        send(s_in.at[t], s_in.at[t], s_sem.at[t], peer_t(k))
    pl.when(~middle)(lambda: window_arrived(2))
    share_near(2)
    for k in range(1, 8):
        at = lax.rem(t + k, 8)
        arrived(s_in.at[at], s_sem.at[at])
    square = s_in[0]
    for k in range(1, 8):
        square = square + s_in[k]
    sx_in[x] = square
    for k in range(1, 4):
        send(sx_in.at[x], sx_in.at[x], sx_sem.at[x], peer_x(k))

    others = [lax.rem(x + k, 4) for k in range(1, 4)]

    def open_side(side):
        for k, at in enumerate(others):
            for b in range(4):
                arrived(x_in.at[at, side, b], x_sem.at[at, side, b])
                code = x_in[at, side, b].astype(F32)
                x_value[side, k, b] = decode(code[:PAIR], code[PAIR:PAIR + 1])

    def factor(sq):
        return (1.0 / jnp.maximum(jnp.sqrt(sq), 1.0))[:1]

    def add_side(side):
        for b in range(4):
            acc = own_factor * bucket_ref[group_at(lax.rem(x + 4 - b, 4)), side, b]
            for k in range(3):
                acc = acc + factors[k] * x_value[side, k, b]
            acc_ref[side, b * ROWS:(b + 1) * ROWS] = acc[:ROWS]
            acc_ref[side, (b + 4) * ROWS:(b + 5) * ROWS] = acc[ROWS:]
        for k in (4, 3, 5, 2, 6, 1, 7):
            rows = pl.ds(pl.multiple_of(lax.rem(y + k, 8) * ROWS, 8), ROWS)
            y_out[side, k - 1] = pack(acc_ref[side, rows], squares)
            send(y_out.at[side, k - 1], y_in.at[side, y], y_sem.at[side, y], peer_y(k))

    def to_owner(side):
        acc = acc_ref[side, pl.ds(pl.multiple_of(y * ROWS, 8), ROWS)]
        s_line[y] = jnp.broadcast_to(squares, (8, BLOCK))
        for k in range(1, 8):
            at = lax.rem(y + k, 8)
            arrived(y_in.at[side, at], y_sem.at[side, at])
            value, line = unpack(y_in[side, at])
            acc = acc + value
            s_line[at] = jnp.broadcast_to(line, (8, BLOCK))
        line = s_line[0]
        for k in range(1, 8):
            line = line + s_line[k]
        p_out[side] = pack(acc, line[:1])
        copy = remote(
            p_out.at[side], p_in.at[zh], p_send.at[side], p_sem.at[zh], device(zl // 2, own_x[side], y, column, q)
        )
        stay = pltpu.make_async_copy(p_out.at[side], p_in.at[zh], p_sem.at[zh])
        pl.when(stays[side])(stay.start)
        pl.when(~stays[side])(copy.start)
        shares.append((~stays[side], copy))

    open_side(0)
    for at in others:
        arrived(sx_in.at[at], sx_sem.at[at])
    squares = (sx_in[0] + sx_in[1] + sx_in[2] + sx_in[3])[:1]
    own_factor = factor(sx_in[x])
    factors = [factor(sx_in[at]) for at in others]
    add_side(0)
    open_side(1)
    add_side(1)
    to_owner(0)
    to_owner(1)
    summed = None
    for k in range(2):
        arrived(p_in.at[k], p_sem.at[k])
        got = unpack(p_in[k])
        summed = got if summed is None else plus(summed, got)
    loads[-1].wait()
    out_ref[...] = SCALE * summed[0] + noise_ref[...]
    mean_ref[...] = jnp.broadcast_to(summed[1] / BATCH, (8, BLOCK))
    for copy in sends:
        copy.wait_send()
    for wanted, copy in shares:
        if wanted is None:
            copy.wait_send()
        else:
            pl.when(wanted)(copy.wait_send)


def shards(hidden_act, out_grad, privacy_noise):
    dma = pltpu.SemaphoreType.DMA
    hbm = pl.BlockSpec(memory_space=pl.ANY)
    vmem = pl.BlockSpec(memory_space=pltpu.VMEM)
    bf16 = jnp.bfloat16
    n_sends = 1 + 2 + 1 + 3 + 7 + 3 + 14
    update, mean = pl.pallas_call(
        kernel,
        out_shape=(pltpu.VMEM((ROWS, BLOCK), F32), pltpu.VMEM((8, BLOCK), F32)),
        in_specs=[hbm, hbm, hbm],
        out_specs=(vmem, vmem),
        scratch_shapes=[
            pltpu.VMEM((SEQ, FF // 8), bf16),
            pltpu.VMEM((OWN, SEQ), bf16),
            pltpu.VMEM((ROWS, BLOCK), F32),
            pltpu.VMEM((OWN, SEQ), bf16),
            pltpu.VMEM((4, SEQ, BLOCK), bf16),
            pltpu.VMEM((2, 4, 2, 3, 32, 128), F32),
            pltpu.VMEM((4, 2, 3, 32, 128), F32),
            pltpu.VMEM((4, 2, 3, 32, 128), F32),
            pltpu.VMEM((3, GRAM + 16, 128), bf16),
            pltpu.VMEM((3, GRAM + 16, 128), bf16),
            pltpu.VMEM((8, 8, 128), F32),
            pltpu.VMEM((4, 2, 4, PAIR, BLOCK), F32),
            pltpu.VMEM((4, 2, 4, CODED, BLOCK), bf16),
            pltpu.VMEM((4, 2, 4, CODED, BLOCK), bf16),
            pltpu.VMEM((2, 3, 4, PAIR, BLOCK), F32),
            pltpu.VMEM((4, 8, 128), F32),
            pltpu.VMEM((8, 8, 128), F32),
            pltpu.VMEM((2, OWN, BLOCK), F32),
            pltpu.VMEM((2, 7, PIECE, BLOCK), bf16),
            pltpu.VMEM((2, 8, PIECE, BLOCK), bf16),
            pltpu.VMEM((2, PIECE, BLOCK), bf16),
            pltpu.VMEM((2, PIECE, BLOCK), bf16),
            dma((CHUNKS + 2,)),
            dma((n_sends,)),
            dma((4, 2, 4)),
            dma((2,)),
            dma((2,)),
            dma((2,)),
            dma((4,)),
            dma((3,)),
            dma((8,)),
            dma((4, 2, 4)),
            dma((4,)),
            dma((2, 8)),
            dma((2,)),
        ],
        compiler_params=pltpu.CompilerParams(
            collective_id=0, has_side_effects=True, vmem_limit_bytes=60 * 2**20
        ),
        cost_estimate=pl.CostEstimate(flops=4 * 10**9, bytes_accessed=5 * 10**6, transcendentals=0),
    )(hidden_act, out_grad.T, privacy_noise)
    return (update, mean[0, 0])


def solution(mesh):
    return jax.shard_map(
        shards,
        mesh=mesh,
        in_specs=(P("dp", "tensor"), P("dp", "tensor"), P("dp", "tensor")),
        out_specs=(P("dp", "tensor"), P()),
        check_vma=False,
    )
```

```python
import math

import jax
import jax.numpy as jnp
from jax import lax
from jax.experimental import pallas as pl
from jax.experimental.pallas import tpu as pltpu
from jax.sharding import PartitionSpec as P

D = 4608
FF = 36864
SEQ = 384
BLOCK = 128
BATCH = 64
OWN = D // 8
ROWS = D // 64
PIECE = ROWS + 8
PAIR = 2 * ROWS
CODED = PAIR + 16
GRAM = 2 * 3 * 32
SPAN = 86.0
CHUNKS = 3
SCALE = math.sqrt(FF * D / BATCH)
F32 = jnp.float32
MESH = pl.DeviceIdType.MESH


def turn_of(group):
    return lax.rem(3 * (group + 4), 5)


def group_at(turn):
    return lax.rem(2 * turn + 1, 5)


def scale_of(value):
    top = jnp.max(jnp.max(jnp.abs(value), axis=0, keepdims=True), axis=1, keepdims=True)
    return (top * 1.01).astype(jnp.bfloat16).astype(F32)


def encode(value, inverse):
    root = jnp.sqrt(jnp.minimum(jnp.abs(value) * inverse, 1.0))
    code = jnp.exp(root * (2 * SPAN) - SPAN)
    return jnp.where(value < 0, -code, code)


def decode(code, scale):
    code = code.astype(F32)
    root = jnp.log(jnp.abs(code)) * (0.5 / SPAN) + 0.5
    value = root * root * scale
    return jnp.where(code < 0, -value, value)


def inverse_of(scale):
    return 1.0 / jnp.maximum(scale, 1e-30)


def pack(value, exact):
    scale = scale_of(value)
    high = exact.astype(jnp.bfloat16).astype(F32)
    middle = (exact - high).astype(jnp.bfloat16).astype(F32)
    low = exact - high - middle
    line = lax.broadcasted_iota(jnp.int32, (8, BLOCK), 0)
    head = jnp.where(line == 0, scale, jnp.where(line == 1, high, jnp.where(line == 2, middle, low)))
    return jnp.concatenate([encode(value, inverse_of(scale)), head], axis=0).astype(jnp.bfloat16)


def unpack(packed):
    packed = packed.astype(F32)
    rows = packed.shape[0] - 8
    head = packed[rows:]
    return decode(packed[:rows], head[:1]), head[1:2] + head[2:3] + head[3:4]


def kernel(
    h_hbm, g_hbm, noise_hbm, out_ref, mean_ref,
    h_ref, g_ref, noise_ref, g_pair, win, a_half, gram_own, pair_recv, gram_out, gram_in, s_in, bucket_ref, x_out, x_in,
    x_value, sx_in, s_line, acc_ref, y_out, y_in, p_out, p_in,
    load_sem, send_sem, x_send, p_send, pass_send, pair_sem, win_sem, gram_sem, s_sem, x_sem, sx_sem, y_sem, p_sem,
):
    dp, t = lax.axis_index("dp"), lax.axis_index("tensor")
    zh, x, y = dp // 32, lax.rem(dp // 8, 4), lax.rem(dp, 8)
    zl, q = t // 2, lax.rem(t, 2)
    column = group_at(lax.rem(x + 8 - y, 4))

    def device(zh_, x_, y_, zl_, q_):
        return (zh_ * 32 + x_ * 8 + y_, zl_ * 2 + q_)

    def peer_z(k):
        return device(zh, x, y, lax.rem(zl + k, 4), q)

    def peer_t(k):
        return (dp, lax.rem(t + k, 8))

    def peer_x(k):
        return device(zh, lax.rem(x + k, 4), y, zl, q)

    def peer_y(k):
        return device(zh, x, lax.rem(y + k, 8), zl, q)

    partner = (dp, t + 1 - 2 * q)
    sends = []

    def remote(src, dst, sent, recv, to):
        return pltpu.make_async_remote_copy(
            src_ref=src, dst_ref=dst, send_sem=sent, recv_sem=recv, device_id=to, device_id_type=MESH
        )

    def send(src, dst, recv, to):
        sends.append(remote(src, dst, send_sem.at[len(sends)], recv, to))
        sends[-1].start()

    def arrived(dst, recv):
        pltpu.make_async_copy(dst, dst, recv).wait()

    barrier = pltpu.get_barrier_semaphore()
    def greet(to):
        pl.semaphore_signal(barrier, inc=1, device_id=to, device_id_type=MESH)

    source_x, source_z = lax.rem(turn_of(zl) + y, 4), zh * 2 + x // 2
    for k in range(2):
        pl.when(~((k == zh) & (source_x == x) & (source_z == zl)))(lambda k=k: greet(device(k, source_x, y, source_z, q)))
    for to in [peer_y(k) for k in range(1, 8)] + [peer_t(k) for k in range(1, 8)] + [peer_x(k) for k in range(1, 4)]:
        greet(to)
    own_x = [lax.rem(zl, 2) * 2 + (q if side == 0 else 1 - q) for side in range(2)]
    stays = [(own_x[side] == x) & (zl // 2 == zh) & (column == zl) for side in range(2)]
    greeted = 17 + sum(1 - stay.astype(jnp.int32) for stay in stays)

    part = h_ref.shape[1] // CHUNKS
    loads = []

    def load(src, dst):
        loads.append(pltpu.make_async_copy(src, dst, load_sem.at[len(loads)]))
        loads[-1].start()

    for c in range(CHUNKS):
        load(h_hbm.at[:, pl.ds(c * part, part)], h_ref.at[:, pl.ds(c * part, part)])
        if c == 0:
            load(g_hbm, g_ref)
    load(noise_hbm, noise_ref)
    def grams(left, right, axis):
        def product(a, b):
            return lax.dot_general(a, b, (((axis,), (axis,)), ((), ())), preferred_element_type=F32)
        return product(left, right(slice(0, 256))), product(right(slice(256, 384)), right(slice(256, 384)))

    def act_term(c):
        columns = slice(c * part, (c + 1) * part)
        return grams(h_ref[:, columns], lambda rows: h_ref[rows, columns], 1)

    def plus(a, b):
        return tuple(i + j for i, j in zip(a, b))

    loads[0].wait()
    win[zl] = h_ref[:, :BLOCK]
    gram = act_term(0)
    pl.semaphore_wait(barrier, greeted)
    low = (zl < 2).astype(jnp.int32)
    near = [zl + 1 - 2 * lax.rem(zl, 2), 1 + low, 3 * low]

    def send_window(to):
        send(win.at[zl], win.at[zl], win_sem.at[zl], device(zh, x, y, to, q))

    middle = (zl == 1) | (zl == 2)
    send_window(near[0])
    send_window(near[1])

    def pass_window(of, to, n):
        copy = remote(win.at[of], win.at[of], pass_send.at[n], win_sem.at[of], device(zh, x, y, to, q))
        pl.when(middle)(copy.start)
        shares.append((middle, copy))

    shares = []
    pass_window(zl, near[2], 0)
    for c in range(1, CHUNKS):
        loads[c + 1].wait()
        gram = plus(gram, act_term(c))
    loads[1].wait()
    grad = grams(g_ref[...], lambda rows: g_ref[:, rows], 0)
    blocks = [(0, 0), (1, 0), (2, 0), (1, 1), (2, 1), (2, 2)]

    def cut(matrices, b, p):
        i, j = blocks[b]
        if b == 5:
            return matrices[1][p * 32:(p + 1) * 32]
        return matrices[0][i * 128 + p * 32:i * 128 + (p + 1) * 32, j * 128:(j + 1) * 128]

    for b in range(6):
        for p in range(4):
            a_half[b // 3, p, 0, b % 3] = cut(gram, b, p)
            a_half[b // 3, p, 1, b % 3] = cut(grad, b, p)
    send(a_half.at[1 - q], pair_recv, pair_sem.at[1], partner)
    send(g_ref, g_pair, pair_sem.at[0], partner)

    def share(slot, side, group):
        bucket = jnp.dot((g_ref, g_pair)[side][...], win[group], preferred_element_type=F32)
        scale = scale_of(bucket)
        inverse = inverse_of(scale)
        tile = jnp.broadcast_to(scale, (16, BLOCK)).astype(jnp.bfloat16)
        for b in range(4):
            rows = slice(b * ROWS, (b + 1) * ROWS), slice((b + 4) * ROWS, (b + 5) * ROWS)
            value = jnp.concatenate([bucket[r] for r in rows], axis=0)
            bucket_ref[group, side, b] = value
            x_out[slot, side, b, :PAIR] = encode(value, inverse).astype(jnp.bfloat16)
            x_out[slot, side, b, PAIR:] = tile
        for k in (1, 3, 2):
            to = lax.rem(x + k, 4)
            b = lax.rem(to + 4 - turn_of(group), 4)
            copy = remote(
                x_out.at[slot, side, b], x_in.at[x, side, b], x_send.at[slot, side, k - 1], x_sem.at[x, side, b],
                device(zh, to, y, zl, q),
            )
            copy.start()
            shares.append((None, copy))

    share(0, 0, zl)
    arrived(pair_recv, pair_sem.at[1])
    gram_own[...] = a_half[q] + pair_recv[...]
    tops = [scale_of(gram_own[:, i].reshape(4 * GRAM // 2, 128)) for i in range(2)]
    for k in range(1, 4):
        to = lax.rem(zl + k, 4)
        for i, top in enumerate(tops):
            code = encode(gram_own[to, i].reshape(GRAM // 2, 128), inverse_of(top))
            gram_out[k - 1, i * GRAM // 2:(i + 1) * GRAM // 2] = code.astype(jnp.bfloat16)
        line = lax.broadcasted_iota(jnp.int32, (16, 128), 0)
        gram_out[k - 1, GRAM:] = jnp.where(line < 8, tops[0], tops[1]).astype(jnp.bfloat16)
        send(gram_out.at[k - 1], gram_in.at[k - 1], gram_sem.at[k - 1], peer_z(k))

    arrived(g_pair, pair_sem.at[0])
    share(0, 1, zl)

    def window_arrived(n):
        arrived(win.at[near[n]], win_sem.at[near[n]])

    def share_near(n):
        for side in range(2):
            share(n + 1, side, near[n])

    window_arrived(0)
    share_near(0)
    window_arrived(1)
    share_near(1)
    pl.when(middle)(lambda: window_arrived(2))
    pass_window(near[2], near[0], 1)

    for k in range(1, 4):
        arrived(gram_in.at[k - 1], gram_sem.at[k - 1])
    total = [gram_own[zl, i] for i in range(2)]
    for k in range(3):
        got = gram_in[k].astype(F32)
        for i in range(2):
            value = decode(got[i * GRAM // 2:(i + 1) * GRAM // 2], got[GRAM + 8 * i:GRAM + 8 * i + 1])
            total[i] = total[i] + value.reshape(3, 32, 128)
    both = total[0] * total[1]
    third = (2 - q).astype(F32)
    weighed = both[0] + 2.0 * both[1] + third * both[2]
    s_in[t] = jnp.full((8, 128), jnp.sum(weighed), F32)
    for k in range(1, 8):
        send(s_in.at[t], s_in.at[t], s_sem.at[t], peer_t(k))
    pl.when(~middle)(lambda: window_arrived(2))
    share_near(2)
    for k in range(1, 8):
        at = lax.rem(t + k, 8)
        arrived(s_in.at[at], s_sem.at[at])
    square = s_in[0]
    for k in range(1, 8):
        square = square + s_in[k]
    sx_in[x] = square
    for k in range(1, 4):
        send(sx_in.at[x], sx_in.at[x], sx_sem.at[x], peer_x(k))

    others = [lax.rem(x + k, 4) for k in range(1, 4)]

    def open_side(side):
        for k, at in enumerate(others):
            for b in range(4):
                arrived(x_in.at[at, side, b], x_sem.at[at, side, b])
                code = x_in[at, side, b].astype(F32)
                x_value[side, k, b] = decode(code[:PAIR], code[PAIR:PAIR + 1])

    def factor(sq):
        return (1.0 / jnp.maximum(jnp.sqrt(sq), 1.0))[:1]

    def add_side(side):
        for b in range(4):
            acc = own_factor * bucket_ref[group_at(lax.rem(x + 4 - b, 4)), side, b]
            for k in range(3):
                acc = acc + factors[k] * x_value[side, k, b]
            acc_ref[side, b * ROWS:(b + 1) * ROWS] = acc[:ROWS]
            acc_ref[side, (b + 4) * ROWS:(b + 5) * ROWS] = acc[ROWS:]
        for k in (4, 3, 5, 2, 6, 1, 7):
            rows = pl.ds(pl.multiple_of(lax.rem(y + k, 8) * ROWS, 8), ROWS)
            y_out[side, k - 1] = pack(acc_ref[side, rows], squares)
            send(y_out.at[side, k - 1], y_in.at[side, y], y_sem.at[side, y], peer_y(k))

    def to_owner(side):
        acc = acc_ref[side, pl.ds(pl.multiple_of(y * ROWS, 8), ROWS)]
        s_line[y] = jnp.broadcast_to(squares, (8, BLOCK))
        for k in range(1, 8):
            at = lax.rem(y + k, 8)
            arrived(y_in.at[side, at], y_sem.at[side, at])
            value, line = unpack(y_in[side, at])
            acc = acc + value
            s_line[at] = jnp.broadcast_to(line, (8, BLOCK))
        line = s_line[0]
        for k in range(1, 8):
            line = line + s_line[k]
        p_out[side] = pack(acc, line[:1])
        copy = remote(
            p_out.at[side], p_in.at[zh], p_send.at[side], p_sem.at[zh], device(zl // 2, own_x[side], y, column, q)
        )
        stay = pltpu.make_async_copy(p_out.at[side], p_in.at[zh], p_sem.at[zh])
        pl.when(stays[side])(stay.start)
        pl.when(~stays[side])(copy.start)
        shares.append((~stays[side], copy))

    open_side(0)
    for at in others:
        arrived(sx_in.at[at], sx_sem.at[at])
    squares = (sx_in[0] + sx_in[1] + sx_in[2] + sx_in[3])[:1]
    own_factor = factor(sx_in[x])
    factors = [factor(sx_in[at]) for at in others]
    add_side(0)
    open_side(1)
    add_side(1)
    to_owner(0)
    to_owner(1)
    summed = None
    for k in range(2):
        arrived(p_in.at[k], p_sem.at[k])
        got = unpack(p_in[k])
        summed = got if summed is None else plus(summed, got)
    loads[-1].wait()
    out_ref[...] = SCALE * summed[0] + noise_ref[...]
    mean_ref[...] = jnp.broadcast_to(summed[1] / BATCH, (8, BLOCK))
    for copy in sends:
        copy.wait_send()
    for wanted, copy in shares:
        if wanted is None:
            copy.wait_send()
        else:
            pl.when(wanted)(copy.wait_send)


def shards(hidden_act, out_grad, privacy_noise):
    dma = pltpu.SemaphoreType.DMA
    hbm = pl.BlockSpec(memory_space=pl.ANY)
    vmem = pl.BlockSpec(memory_space=pltpu.VMEM)
    bf16 = jnp.bfloat16
    n_sends = 1 + 2 + 1 + 3 + 7 + 3 + 14
    update, mean = pl.pallas_call(
        kernel,
        out_shape=(pltpu.VMEM((ROWS, BLOCK), F32), pltpu.VMEM((8, BLOCK), F32)),
        in_specs=[hbm, hbm, hbm],
        out_specs=(vmem, vmem),
        scratch_shapes=[
            pltpu.VMEM((SEQ, FF // 8), bf16),
            pltpu.VMEM((OWN, SEQ), bf16),
            pltpu.VMEM((ROWS, BLOCK), F32),
            pltpu.VMEM((OWN, SEQ), bf16),
            pltpu.VMEM((4, SEQ, BLOCK), bf16),
            pltpu.VMEM((2, 4, 2, 3, 32, 128), F32),
            pltpu.VMEM((4, 2, 3, 32, 128), F32),
            pltpu.VMEM((4, 2, 3, 32, 128), F32),
            pltpu.VMEM((3, GRAM + 16, 128), bf16),
            pltpu.VMEM((3, GRAM + 16, 128), bf16),
            pltpu.VMEM((8, 8, 128), F32),
            pltpu.VMEM((4, 2, 4, PAIR, BLOCK), F32),
            pltpu.VMEM((4, 2, 4, CODED, BLOCK), bf16),
            pltpu.VMEM((4, 2, 4, CODED, BLOCK), bf16),
            pltpu.VMEM((2, 3, 4, PAIR, BLOCK), F32),
            pltpu.VMEM((4, 8, 128), F32),
            pltpu.VMEM((8, 8, 128), F32),
            pltpu.VMEM((2, OWN, BLOCK), F32),
            pltpu.VMEM((2, 7, PIECE, BLOCK), bf16),
            pltpu.VMEM((2, 8, PIECE, BLOCK), bf16),
            pltpu.VMEM((2, PIECE, BLOCK), bf16),
            pltpu.VMEM((2, PIECE, BLOCK), bf16),
            dma((CHUNKS + 2,)),
            dma((n_sends,)),
            dma((4, 2, 4)),
            dma((2,)),
            dma((2,)),
            dma((2,)),
            dma((4,)),
            dma((3,)),
            dma((8,)),
            dma((4, 2, 4)),
            dma((4,)),
            dma((2, 8)),
            dma((2,)),
        ],
        compiler_params=pltpu.CompilerParams(
            collective_id=0, has_side_effects=True, vmem_limit_bytes=60 * 2**20
        ),
        cost_estimate=pl.CostEstimate(flops=4 * 10**9, bytes_accessed=5 * 10**6, transcendentals=0),
    )(hidden_act, out_grad.T, privacy_noise)
    return (update, mean[0, 0])


def solution(mesh):
    return jax.shard_map(
        shards,
        mesh=mesh,
        in_specs=(P("dp", "tensor"), P("dp", "tensor"), P("dp", "tensor")),
        out_specs=(P("dp", "tensor"), P()),
        check_vma=False,
    )
```
